256 devices in a mesh: grp: 32 (over z, x), sp: 8 (over y, core).
Axes of the slice: x: 4, y: 4, z: 8, core: 2. Of those that a mesh axis runs over, the one named last changes fastest.
Arguments:
- query_rows: bfloat16 [32, 8, 32, 8, 5120], P('grp', 'sp'), may hold values from -8 to 8
- key_rows: bfloat16 [32, 8, 32, 8, 1024], P('grp', 'sp'), may hold values from -6 to 6
- value_row_array: bfloat16 [32, 8, 32, 8, 1024], P('grp', 'sp'), may hold values from -6 to 6
- lengths: int32 [32, 2], P('grp'), may hold values from 0 to 2048, as said below
Outputs:
- attended: bfloat16 [32, 8, 32, 8, 5120], P('grp', 'sp')
The draws below stay inside these ranges and needn't reach their ends.
Inputs may be any that keep to these rules, and one draw needn't show every extreme that they name: `lengths`: each group holds either one sequence of 2048 rows (second length 0) or two sequences of 1024 rows; both kinds occur in every draw.
All inputs are finite; a program needn't handle non-finite values.
Results may differ from the reference program's by a relative error of at most 0.007.
Values may be sent and summed in bfloat16 or wider, within the bound.
A program may use at most 64 MiB of HBM per device.

```python
import jax
import jax.numpy as jnp
from jax import lax

QUERY_HEAD_COUNT = 40
KEY_VALUE_HEADS = 8
HEAD_SIZE = 128
LOADER_PIECE = 8
GROUP_TOKENS = 2048
N_GRP = 32
N_SP = 8


def draw_query_rows(key, part):
    key = jax.random.fold_in(key, 11)
    array_shape = (N_GRP, N_SP, N_GRP, LOADER_PIECE, QUERY_HEAD_COUNT * HEAD_SIZE)
    value_matrix = jnp.clip(jax.random.normal(key, array_shape, jnp.float32), -6.0, 6.0)
    return value_matrix.astype(jnp.bfloat16)


def draw_key_rows(key, part):
    key = jax.random.fold_in(key, 23)
    array_shape = (N_GRP, N_SP, N_GRP, LOADER_PIECE, KEY_VALUE_HEADS * HEAD_SIZE)
    value_matrix = jnp.clip(jax.random.normal(key, array_shape, jnp.float32), -6.0, 6.0)
    return value_matrix.astype(jnp.bfloat16)


def draw_lengths(key, part):
    key = jax.random.fold_in(key, 37)
    single = jax.random.randint(key, (N_GRP,), 0, 2, jnp.int32)
    places = jnp.arange(N_GRP, dtype=jnp.int32)
    single = jnp.where(places == 0, 1, jnp.where(places == 1, 0, single))
    first = jnp.where(single == 1, GROUP_TOKENS, GROUP_TOKENS // 2).astype(jnp.int32)
    second = (GROUP_TOKENS - first).astype(jnp.int32)
    return jnp.stack([first, second], axis=1)


def block_levels(own_key, dims, pieces, low, top_value):
    def one(position, parts):
        draws = jax.random.uniform(jax.random.fold_in(jax.random.fold_in(own_key, 6), position), (parts,), jnp.float32, low / len(pieces), top_value / len(pieces))
        return jnp.repeat(jnp.exp(draws), dims[position] // parts).reshape((-1,) + (1,) * (len(dims) - position - 1))

    level = one(*pieces[0])
    for cut in pieces[1:]:
        level = level * one(*cut)
    return level


def gaussian(own_key, dims, spread, limit, cuts=(), kind=jnp.bfloat16):
    loudness = block_levels(own_key, dims, cuts, -0.22, 0.18) if cuts else 1.0
    values = jax.random.normal(own_key, dims, jnp.float32) * spread * loudness
    return jnp.minimum(jnp.maximum(values, -limit), limit).astype(kind)


def setup_inputs(seed: int = 0) -> dict:
    arg_keys = jax.random.split(jax.random.key(seed), 5)
    query_rows = draw_query_rows(jax.random.fold_in(arg_keys[4], 71), 0)
    key_rows = draw_key_rows(jax.random.fold_in(arg_keys[4], 71), 0)
    value_row_array = gaussian(arg_keys[2], (N_GRP, N_SP, N_GRP, LOADER_PIECE, KEY_VALUE_HEADS * HEAD_SIZE), 1.0, 6.0, ((0, 32), (1, 8)))
    lengths = draw_lengths(jax.random.fold_in(arg_keys[4], 71), 0)
    return {"query_rows": query_rows, "key_rows": key_rows, "value_row_array": value_row_array, "lengths": lengths}


def to_buffer(loader_rows):
    return loader_rows.transpose(2, 0, 1, 3, 4).reshape(N_GRP, GROUP_TOKENS, loader_rows.shape[4])


def segment_ids(lengths):
    ends = jnp.cumsum(lengths, axis=1)
    places = jnp.arange(GROUP_TOKENS, dtype=jnp.int32)
    return jnp.sum((places[None, :, None] >= ends[:, None, :]).astype(jnp.int32), axis=2)


def attend_group(operands):
    query_matrix, key_matrix, value_matrix, segment = operands
    places = jnp.arange(GROUP_TOKENS, dtype=jnp.int32)
    allowed = (places[None, :] <= places[:, None]) & (segment[None, :] == segment[:, None])
    query_matrix = query_matrix.reshape(GROUP_TOKENS, KEY_VALUE_HEADS, QUERY_HEAD_COUNT // KEY_VALUE_HEADS, HEAD_SIZE).transpose(1, 0, 2, 3)
    key_matrix = key_matrix.reshape(GROUP_TOKENS, KEY_VALUE_HEADS, HEAD_SIZE).transpose(1, 0, 2)
    value_matrix = value_matrix.reshape(GROUP_TOKENS, KEY_VALUE_HEADS, HEAD_SIZE).transpose(1, 0, 2)

    def attend_head(head_operands):
        head_query, head_key, head_value = head_operands
        scores = jnp.einsum("tgd,ud->gtu", head_query.astype(jnp.float32), head_key.astype(jnp.float32)) * HEAD_SIZE ** -0.5
        scores = jnp.where(allowed[None], scores, -jnp.inf)
        highest = jnp.max(scores, axis=2, keepdims=True)
        expo = jnp.exp(scores - highest)
        total_sum = jnp.sum(expo, axis=2)
        weights = lax.optimization_barrier(expo.astype(jnp.bfloat16))
        blended = jnp.einsum("gtu,ud->tgd", weights.astype(jnp.float32), head_value.astype(jnp.float32))
        return blended / total_sum.T[:, :, None]

    per_head = lax.map(attend_head, (query_matrix, key_matrix, value_matrix))
    return per_head.transpose(1, 0, 2, 3).reshape(GROUP_TOKENS, QUERY_HEAD_COUNT * HEAD_SIZE).astype(jnp.bfloat16)


def reference(query_rows, key_rows, value_row_array, lengths):
    segment = segment_ids(lengths)
    mixed = lax.map(attend_group, (to_buffer(query_rows), to_buffer(key_rows), to_buffer(value_row_array), segment))
    return mixed.reshape(N_GRP, N_GRP, N_SP, LOADER_PIECE, QUERY_HEAD_COUNT * HEAD_SIZE).transpose(1, 2, 0, 3, 4)
```

```python
import functools

import jax
import jax.numpy as jnp
from jax import lax
from jax.experimental import pallas as pl
from jax.experimental.pallas import tpu as pltpu
from jax.sharding import PartitionSpec as P

MESH = pl.DeviceIdType.MESH
HEAD = 128
RATIO = 5
HEADS = 8
PLANES = 8
MEMBERS = 32
PIECE = 8
ROWS = MEMBERS * PIECE
QW = RATIO * HEAD
HALF = 1024
FAR = 1e30
RATE = HEAD**-0.5 * 1.4426950408889634


def member(plane, j):
    return (plane * 4 + j // 8, j % 8)


def kernel(
    q_ref,
    k_ref,
    v_ref,
    len_ref,
    out_ref,
    qbuf,
    kv,
    obuf,
    ends,
    qh,
    top,
    total,
    acc,
    q_send,
    q_recv,
    kv_send,
    kv_recv,
    z_send,
    z_recv,
    o_send,
    o_recv,
    l_send,
    l_recv,
):
    g, s = lax.axis_index("grp"), lax.axis_index("sp")
    z, j = g // 4, (g % 4) * 8 + s
    up, down = member((z + 1) % 8, j), member((z + 7) % 8, j)

    barrier = pltpu.get_barrier_semaphore()

    def greet(i, _):
        pl.semaphore_signal(
            barrier, inc=1, device_id=member(z, (j + i) % MEMBERS), device_id_type=MESH
        )
        return 0

    lax.fori_loop(1, MEMBERS, greet, 0)
    pl.semaphore_signal(barrier, inc=1, device_id=up, device_id_type=MESH)
    pl.semaphore_signal(barrier, inc=1, device_id=down, device_id_type=MESH)
    to_plane, to_j = s, g
    alone = jnp.logical_and(to_plane == z, to_j == j)

    @pl.when(jnp.logical_not(alone))
    def _():
        pl.semaphore_signal(barrier, inc=1, device_id=(j, z), device_id_type=MESH)
        pl.semaphore_wait(barrier, MEMBERS + 2)

    @pl.when(alone)
    def _():
        pl.semaphore_wait(barrier, MEMBERS + 1)

    def send_kv(m):
        cols = pl.ds(pl.multiple_of(m * HEAD, HEAD), HEAD)

        def one(i, _):
            p = (j + i) % MEMBERS
            for n, ref in enumerate((k_ref, v_ref)):
                pltpu.make_async_remote_copy(
                    src_ref=ref.at[0, 0, p, :, cols],
                    dst_ref=kv.at[z, m, n, j],
                    send_sem=kv_send,
                    recv_sem=kv_recv.at[m],
                    device_id=member(z, p),
                    device_id_type=MESH,
                ).start()
            return 0

        lax.fori_loop(1, MEMBERS, one, 0)
        for n, ref in enumerate((k_ref, v_ref)):
            pltpu.make_async_copy(
                ref.at[0, 0, j, :, cols], kv.at[z, m, n, j], kv_recv.at[m]
            ).start()

    def send_q(m):
        cols = pl.ds(pl.multiple_of(m * QW, HEAD), QW)

        def one(i, _):
            p = (j + i) % MEMBERS
            pltpu.make_async_remote_copy(
                src_ref=q_ref.at[0, 0, p, :, cols],
                dst_ref=qbuf.at[m, j],
                send_sem=q_send,
                recv_sem=q_recv.at[m],
                device_id=member(z, p),
                device_id_type=MESH,
            ).start()
            return 0

        lax.fori_loop(1, MEMBERS, one, 0)
        pltpu.make_async_copy(
            q_ref.at[0, 0, j, :, cols], qbuf.at[m, j], q_recv.at[m]
        ).start()

    def send_out(m):
        cols = pl.ds(pl.multiple_of(m * QW, HEAD), QW)

        def one(i, _):
            p = (j + i) % MEMBERS
            pltpu.make_async_remote_copy(
                src_ref=obuf.at[m, p],
                dst_ref=out_ref.at[0, 0, j, :, cols],
                send_sem=o_send,
                recv_sem=o_recv,
                device_id=member(z, p),
                device_id_type=MESH,
            ).start()
            return 0

        lax.fori_loop(1, MEMBERS, one, 0)
        pltpu.make_async_copy(
            obuf.at[m, j], out_ref.at[0, 0, j, :, cols], o_recv
        ).start()

    def wait_bytes(ref, sem):
        pltpu.make_async_copy(ref, ref, sem).wait()

    def ups(m):
        return 4 - m % 2

    def up_copy(b, m, hop):
        return pltpu.make_async_remote_copy(
            src_ref=kv.at[b, m],
            dst_ref=kv.at[b, m],
            send_sem=z_send.at[0, hop, m],
            recv_sem=z_recv.at[0, hop, m],
            device_id=up,
            device_id_type=MESH,
        )

    def down_copy(b, m, hop):
        return pltpu.make_async_remote_copy(
            src_ref=kv.at[b, m],
            dst_ref=kv.at[b, m],
            send_sem=z_send.at[1, hop, m],
            recv_sem=z_recv.at[1, hop, m],
            device_id=down,
            device_id_type=MESH,
        )

    def inside(m):
        return jnp.logical_and(m >= 0, m < HEADS)

    def all_of(*conditions):
        return functools.reduce(jnp.logical_and, conditions)

    def sends_up(m, hop):
        return all_of(inside(m), z < 7, z - hop >= 0, hop < ups(m))

    def sends_down(m, hop):
        return all_of(inside(m), (z + hop) % 8 < 7 - ups(m), hop < 7 - ups(m))

    def gets_up(m, hop):
        return all_of(inside(m), z - hop - 1 >= 0, hop < ups(m))

    def gets_down(m, hop):
        return all_of(inside(m), (z + hop + 1) % 8 < 7 - ups(m), hop < 7 - ups(m))

    def flat(x):
        return x.astype(jnp.float32).reshape(ROWS, HEAD).astype(jnp.bfloat16)

    ones = jnp.ones((ROWS, HEAD), jnp.bfloat16)

    def scores_of(m, i, keys):
        return lax.dot_general(
            qh[m, i], keys, (((1,), (1,)), ((), ())), preferred_element_type=jnp.float32
        )

    def attend_own(m):
        keys = flat(kv[z, m, 0])
        values = jnp.concatenate([flat(kv[z, m, 1]), ones], axis=1)
        rows = lax.broadcasted_iota(jnp.int32, (ROWS, ROWS), 0)
        columns = lax.broadcasted_iota(jnp.int32, (ROWS, ROWS), 1)
        for i in range(RATIO):
            qh[m, i] = flat(qbuf[m, :, :, i * HEAD : (i + 1) * HEAD])
            scores = jnp.where(columns <= rows, scores_of(m, i, keys), -FAR)
            highest = jnp.max(scores, axis=1, keepdims=True)
            weights = jnp.exp2((scores - highest) * RATE).astype(jnp.bfloat16)
            both = jnp.dot(weights, values, preferred_element_type=jnp.float32)
            top[m, i] = jnp.broadcast_to(highest, (ROWS, HEAD))
            acc[m, i] = both[:, :HEAD]
            total[m, i] = both[:, HEAD:]

    def attend(m, b):
        keys = flat(kv[b, m, 0])
        values = jnp.concatenate([flat(kv[b, m, 1]), ones], axis=1)
        across = jnp.logical_and(z >= 4, b < 4).astype(jnp.int32)
        hidden = jnp.where(ends[0:1, :] * across == HALF, -FAR, 0.0)
        for i in range(RATIO):
            scores = scores_of(m, i, keys)
            old = top[m, i]
            highest = jnp.max(scores, axis=1, keepdims=True) + hidden
            new = jnp.maximum(old, highest)
            shift = new - hidden
            weights = jnp.exp2(
                (scores - jnp.concatenate([shift, shift], axis=1)) * RATE
            ).astype(jnp.bfloat16)
            both = jnp.dot(weights, values, preferred_element_type=jnp.float32)
            shrink = jnp.exp2((old - new) * RATE)
            top[m, i] = new
            acc[m, i] = acc[m, i] * shrink + both[:, :HEAD]
            total[m, i] = total[m, i] * shrink + both[:, HEAD:]

    def finish(m):
        for i in range(RATIO):
            mixed = acc[m, i] / total[m, i]
            obuf[m, :, :, i * HEAD : (i + 1) * HEAD] = mixed.reshape(
                MEMBERS, PIECE, HEAD
            ).astype(jnp.bfloat16)

    len_copy = pltpu.make_async_remote_copy(
        src_ref=len_ref,
        dst_ref=ends,
        send_sem=l_send,
        recv_sem=l_recv,
        device_id=member(to_plane, to_j),
        device_id_type=MESH,
    )

    send_kv(0)

    @pl.when(jnp.logical_not(alone))
    def _():
        len_copy.start()

    @pl.when(alone)
    def _():
        pltpu.make_async_copy(len_ref, ends, l_recv).start()

    send_kv(1)
    send_q(0)

    def tick(t, _):
        @pl.when(t < HEADS)
        def _():
            wait_bytes(kv.at[z, t], kv_recv.at[t])

            @pl.when(sends_up(t, 0))
            def _():
                up_copy(z, t, 0).start()

            @pl.when(sends_down(t, 0))
            def _():
                down_copy(z, t, 0).start()

        @pl.when(t + 2 < HEADS)
        def _():
            send_kv(t + 2)

        @pl.when(t + 1 < HEADS)
        def _():
            send_q(t + 1)

        @pl.when(t == 0)
        def _():
            wait_bytes(ends, l_recv)

        def hop_step(r, _):
            hop = 3 - r
            m = t - 1 - hop
            from_up = z - hop - 1
            from_down = (z + hop + 1) % 8

            @pl.when(gets_up(m, hop))
            def _():
                up_copy(from_up, m, hop).wait_recv()

                @pl.when(sends_up(m, hop + 1))
                def _():
                    up_copy(from_up, m, hop + 1).start()

            @pl.when(gets_down(m, hop))
            def _():
                down_copy(from_down, m, hop).wait_recv()

                @pl.when(sends_down(m, hop + 1))
                def _():
                    down_copy(from_down, m, hop + 1).start()

            @pl.when(gets_up(m, hop))
            def _():
                attend(m, from_up)

            @pl.when(jnp.logical_and(gets_down(m, hop), from_down < z))
            def _():
                attend(m, from_down)

            return 0

        lax.fori_loop(0, 4, hop_step, 0)

        @pl.when(t >= 4)
        def _():
            finish(t - 4)
            send_out(t - 4)

        @pl.when(t < HEADS)
        def _():
            wait_bytes(qbuf.at[t], q_recv.at[t])
            attend_own(t)

        return 0

    lax.fori_loop(0, HEADS + 4, tick, 0)

    def drain(m, _):
        for hop in range(4):

            @pl.when(sends_up(m, hop))
            def _():
                up_copy(z, m, hop).wait_send()

            @pl.when(sends_down(m, hop))
            def _():
                down_copy(z, m, hop).wait_send()

        return 0

    lax.fori_loop(0, HEADS, drain, 0)

    @pl.when(jnp.logical_not(alone))
    def _():
        len_copy.wait_send()

    wait_bytes(kv.at[0, :, :, pl.ds(0, MEMBERS - 1)], kv_send)
    wait_bytes(qbuf.at[:, pl.ds(0, MEMBERS - 1)], q_send)
    wait_bytes(obuf.at[:, pl.ds(0, MEMBERS - 1)], o_send)
    wait_bytes(out_ref, o_recv)


def on_device(query_rows, key_rows, value_row_array, lengths):
    first = jnp.broadcast_to(lengths[0, 0], (8, HEAD))
    anywhere = pl.BlockSpec(memory_space=pl.ANY)
    dma = pltpu.SemaphoreType.DMA
    pairs = ROWS * ROWS * 8
    return pl.pallas_call(
        kernel,
        out_shape=jax.ShapeDtypeStruct(query_rows.shape, query_rows.dtype),
        in_specs=[anywhere, anywhere, anywhere, pl.BlockSpec(memory_space=pltpu.VMEM)],
        out_specs=anywhere,
        scratch_shapes=[
            pltpu.VMEM((HEADS, MEMBERS, PIECE, QW), jnp.bfloat16),
            pltpu.VMEM((PLANES, HEADS, 2, MEMBERS, PIECE, HEAD), jnp.bfloat16),
            pltpu.VMEM((HEADS, MEMBERS, PIECE, QW), jnp.bfloat16),
            pltpu.VMEM((8, HEAD), jnp.int32),
            pltpu.VMEM((HEADS, RATIO, ROWS, HEAD), jnp.bfloat16),
            pltpu.VMEM((HEADS, RATIO, ROWS, HEAD), jnp.float32),
            pltpu.VMEM((HEADS, RATIO, ROWS, HEAD), jnp.float32),
            pltpu.VMEM((HEADS, RATIO, ROWS, HEAD), jnp.float32),
            dma,
            dma((HEADS,)),
            dma,
            dma((HEADS,)),
            dma((2, 4, HEADS)),
            dma((2, 4, HEADS)),
            dma,
            dma,
            dma,
            dma,
        ],
        compiler_params=pltpu.CompilerParams(
            collective_id=0, has_side_effects=True, vmem_limit_bytes=48 << 20
        ),
        cost_estimate=pl.CostEstimate(
            flops=pairs * HEADS * RATIO * HEAD * 4,
            bytes_accessed=16 << 20,
            transcendentals=pairs * HEADS * RATIO,
        ),
        name="attend_plane",
    )(query_rows, key_rows, value_row_array, first)


def solution(mesh):
    rows = P("grp", "sp", None, None, None)
    return jax.shard_map(
        on_device,
        mesh=mesh,
        in_specs=(rows, rows, rows, P("grp", None)),
        out_specs=rows,
        check_vma=False,
    )
```

```python
import functools

import jax
import jax.numpy as jnp
from jax import lax
from jax.experimental import pallas as pl
from jax.experimental.pallas import tpu as pltpu
from jax.sharding import PartitionSpec as P

MESH = pl.DeviceIdType.MESH
HEAD = 128
RATIO = 5
HEADS = 8
PLANES = 8
MEMBERS = 32
PIECE = 8
ROWS = MEMBERS * PIECE
QW = RATIO * HEAD
HALF = 1024
FAR = 1e30
RATE = HEAD**-0.5 * 1.4426950408889634


def member(plane, j):
    return (plane * 4 + j // 8, j % 8)


def kernel(
    q_ref,
    k_ref,
    v_ref,
    len_ref,
    out_ref,
    qbuf,
    kv,
    obuf,
    ends,
    qh,
    top,
    total,
    acc,
    q_send,
    q_recv,
    kv_send,
    kv_recv,
    z_send,
    z_recv,
    o_send,
    o_recv,
    l_send,
    l_recv,
):
    g, s = lax.axis_index("grp"), lax.axis_index("sp")
    z, j = g // 4, (g % 4) * 8 + s
    up, down = member((z + 1) % 8, j), member((z + 7) % 8, j)

    barrier = pltpu.get_barrier_semaphore()

    def greet(i, _):
        pl.semaphore_signal(
            barrier, inc=1, device_id=member(z, (j + i) % MEMBERS), device_id_type=MESH
        )
        return 0

    lax.fori_loop(1, MEMBERS, greet, 0)
    pl.semaphore_signal(barrier, inc=1, device_id=up, device_id_type=MESH)
    pl.semaphore_signal(barrier, inc=1, device_id=down, device_id_type=MESH)
    to_plane, to_j = s, g
    alone = jnp.logical_and(to_plane == z, to_j == j)

    @pl.when(jnp.logical_not(alone))
    def _():
        pl.semaphore_signal(barrier, inc=1, device_id=(j, z), device_id_type=MESH)
        pl.semaphore_wait(barrier, MEMBERS + 2)

    @pl.when(alone)
    def _():
        pl.semaphore_wait(barrier, MEMBERS + 1)

    def send_kv(m):
        cols = pl.ds(pl.multiple_of(m * HEAD, HEAD), HEAD)

        def one(i, _):
            p = (j + i) % MEMBERS
            for n, ref in enumerate((k_ref, v_ref)):
                pltpu.make_async_remote_copy(
                    src_ref=ref.at[0, 0, p, :, cols],
                    dst_ref=kv.at[z, m, n, j],
                    send_sem=kv_send,
                    recv_sem=kv_recv.at[m],
                    device_id=member(z, p),
                    device_id_type=MESH,
                ).start()
            return 0

        lax.fori_loop(1, MEMBERS, one, 0)
        for n, ref in enumerate((k_ref, v_ref)):
            pltpu.make_async_copy(
                ref.at[0, 0, j, :, cols], kv.at[z, m, n, j], kv_recv.at[m]
            ).start()

    def send_q(m):
        cols = pl.ds(pl.multiple_of(m * QW, HEAD), QW)

        def one(i, _):
            p = (j + i) % MEMBERS
            pltpu.make_async_remote_copy(
                src_ref=q_ref.at[0, 0, p, :, cols],
                dst_ref=qbuf.at[m, j],
                send_sem=q_send,
                recv_sem=q_recv.at[m],
                device_id=member(z, p),
                device_id_type=MESH,
            ).start()
            return 0

        lax.fori_loop(1, MEMBERS, one, 0)
        pltpu.make_async_copy(
            q_ref.at[0, 0, j, :, cols], qbuf.at[m, j], q_recv.at[m]
        ).start()

    def send_out(m):
        cols = pl.ds(pl.multiple_of(m * QW, HEAD), QW)

        def one(i, _):
            p = (j + i) % MEMBERS
            pltpu.make_async_remote_copy(
                src_ref=obuf.at[m, p],
                dst_ref=out_ref.at[0, 0, j, :, cols],
                send_sem=o_send,
                recv_sem=o_recv,
                device_id=member(z, p),
                device_id_type=MESH,
            ).start()
            return 0

        lax.fori_loop(1, MEMBERS, one, 0)
        pltpu.make_async_copy(
            obuf.at[m, j], out_ref.at[0, 0, j, :, cols], o_recv
        ).start()

    def wait_bytes(ref, sem):
        pltpu.make_async_copy(ref, ref, sem).wait()

    def up_copy(b, m, hop):
        return pltpu.make_async_remote_copy(
            src_ref=kv.at[b, m],
            dst_ref=kv.at[b, m],
            send_sem=z_send.at[0, hop, m],
            recv_sem=z_recv.at[0, hop, m],
            device_id=up,
            device_id_type=MESH,
        )

    def down_copy(b, m, hop):
        return pltpu.make_async_remote_copy(
            src_ref=kv.at[b, m],
            dst_ref=kv.at[b, m],
            send_sem=z_send.at[1, hop, m],
            recv_sem=z_recv.at[1, hop, m],
            device_id=down,
            device_id_type=MESH,
        )

    def inside(m):
        return jnp.logical_and(m >= 0, m < HEADS)

    def all_of(*conditions):
        return functools.reduce(jnp.logical_and, conditions)

    def goes_up(b, m, hop):
        turn = all_of(hop == 3, b == 3, m % 2 == 0)
        return all_of(inside(m), b >= 0, b + hop < 7, jnp.logical_or(hop < 3, turn))

    def goes_down(b, m, hop):
        turn = jnp.logical_and(b == 3, m % 2 == 1)
        return all_of(inside(m), hop < 4, jnp.logical_or(b < 3, turn))

    def sends_up(m, hop):
        return goes_up(z - hop, m, hop)

    def sends_down(m, hop):
        return goes_down((z + hop) % 8, m, hop)

    def gets_up(m, hop):
        return goes_up(z - hop - 1, m, hop)

    def gets_down(m, hop):
        return goes_down((z + hop + 1) % 8, m, hop)

    def start_own(m):
        wait_bytes(kv.at[z, m], kv_recv.at[m])

        @pl.when(sends_up(m, 0))
        def _():
            up_copy(z, m, 0).start()

        @pl.when(sends_down(m, 0))
        def _():
            down_copy(z, m, 0).start()

    def flat(x):
        return x.astype(jnp.float32).reshape(ROWS, HEAD).astype(jnp.bfloat16)

    ones = jnp.ones((ROWS, HEAD), jnp.bfloat16)

    def scores_of(m, i, keys):
        return lax.dot_general(
            qh[m, i], keys, (((1,), (1,)), ((), ())), preferred_element_type=jnp.float32
        )

    def attend_own(m):
        keys = flat(kv[z, m, 0])
        values = jnp.concatenate([flat(kv[z, m, 1]), ones], axis=1)
        rows = lax.broadcasted_iota(jnp.int32, (ROWS, ROWS), 0)
        columns = lax.broadcasted_iota(jnp.int32, (ROWS, ROWS), 1)
        for i in range(RATIO):
            qh[m, i] = flat(qbuf[m, :, :, i * HEAD : (i + 1) * HEAD])
            scores = jnp.where(columns <= rows, scores_of(m, i, keys), -FAR)
            highest = jnp.max(scores, axis=1, keepdims=True)
            weights = jnp.exp2((scores - highest) * RATE).astype(jnp.bfloat16)
            both = jnp.dot(weights, values, preferred_element_type=jnp.float32)
            top[m, i] = jnp.broadcast_to(highest, (ROWS, HEAD))
            acc[m, i] = both[:, :HEAD]
            total[m, i] = both[:, HEAD:]

    def attend(m, b):
        keys = flat(kv[b, m, 0])
        values = jnp.concatenate([flat(kv[b, m, 1]), ones], axis=1)
        across = jnp.logical_and(z >= 4, b < 4).astype(jnp.int32)
        first = jnp.broadcast_to(ends[0:1, 0:1], (1, HEAD))
        hidden = jnp.where(first * across == HALF, -FAR, 0.0)
        for i in range(RATIO):
            scores = scores_of(m, i, keys)
            old = top[m, i]
            highest = jnp.max(scores, axis=1, keepdims=True) + hidden
            new = jnp.maximum(old, highest)
            shift = new - hidden
            weights = jnp.exp2(
                (scores - jnp.concatenate([shift, shift], axis=1)) * RATE
            ).astype(jnp.bfloat16)
            both = jnp.dot(weights, values, preferred_element_type=jnp.float32)
            shrink = jnp.exp2((old - new) * RATE)
            top[m, i] = new
            acc[m, i] = acc[m, i] * shrink + both[:, :HEAD]
            total[m, i] = total[m, i] * shrink + both[:, HEAD:]

    def finish(m):
        for i in range(RATIO):
            mixed = acc[m, i] / total[m, i]
            obuf[m, :, :, i * HEAD : (i + 1) * HEAD] = mixed.reshape(
                MEMBERS, PIECE, HEAD
            ).astype(jnp.bfloat16)

    len_copy = pltpu.make_async_remote_copy(
        src_ref=len_ref,
        dst_ref=ends,
        send_sem=l_send,
        recv_sem=l_recv,
        device_id=member(to_plane, to_j),
        device_id_type=MESH,
    )

    send_kv(0)

    @pl.when(jnp.logical_not(alone))
    def _():
        len_copy.start()

    @pl.when(alone)
    def _():
        pltpu.make_async_copy(len_ref, ends, l_recv).start()

    send_kv(1)
    send_q(0)
    send_kv(2)
    send_q(1)
    send_kv(3)
    start_own(0)

    def tick(t, _):
        @pl.when(t + 1 < HEADS)
        def _():
            start_own(t + 1)

        @pl.when(t == 0)
        def _():
            wait_bytes(ends, l_recv)

        def hop_step(hop, _):
            m = t - 1 - hop
            from_up = z - hop - 1
            from_down = (z + hop + 1) % 8

            @pl.when(gets_up(m, hop))
            def _():
                up_copy(from_up, m, hop).wait_recv()

                @pl.when(sends_up(m, hop + 1))
                def _():
                    up_copy(from_up, m, hop + 1).start()

            @pl.when(gets_down(m, hop))
            def _():
                down_copy(from_down, m, hop).wait_recv()

                @pl.when(sends_down(m, hop + 1))
                def _():
                    down_copy(from_down, m, hop + 1).start()

            @pl.when(jnp.logical_and(hop == 0, inside(t - 1)))
            def _():
                wait_bytes(qbuf.at[t - 1], q_recv.at[t - 1])
                attend_own(t - 1)

            @pl.when(gets_up(m, hop))
            def _():
                attend(m, from_up)

            @pl.when(jnp.logical_and(gets_down(m, hop), from_down < z))
            def _():
                attend(m, from_down)

            return 0

        lax.fori_loop(0, 4, hop_step, 0)

        @pl.when(t + 4 < HEADS)
        def _():
            send_kv(t + 4)

        @pl.when(t + 2 < HEADS)
        def _():
            send_q(t + 2)

        @pl.when(t >= 4)
        def _():
            finish(t - 4)
            send_out(t - 4)

        return 0

    lax.fori_loop(0, HEADS + 4, tick, 0)

    def drain(m, _):
        for hop in range(4):

            @pl.when(sends_up(m, hop))
            def _():
                up_copy(z, m, hop).wait_send()

            @pl.when(sends_down(m, hop))
            def _():
                down_copy(z, m, hop).wait_send()

        return 0

    lax.fori_loop(0, HEADS, drain, 0)

    @pl.when(jnp.logical_not(alone))
    def _():
        len_copy.wait_send()

    wait_bytes(kv.at[0, :, :, pl.ds(0, MEMBERS - 1)], kv_send)
    wait_bytes(qbuf.at[:, pl.ds(0, MEMBERS - 1)], q_send)
    wait_bytes(obuf.at[:, pl.ds(0, MEMBERS - 1)], o_send)
    wait_bytes(out_ref, o_recv)


def on_device(query_rows, key_rows, value_row_array, lengths):
    anywhere = pl.BlockSpec(memory_space=pl.ANY)
    there = pl.BlockSpec(memory_space=pltpu.HBM)
    dma = pltpu.SemaphoreType.DMA
    pairs = ROWS * ROWS * 8
    return pl.pallas_call(
        kernel,
        out_shape=jax.ShapeDtypeStruct(query_rows.shape, query_rows.dtype),
        in_specs=[there] * 4,
        out_specs=anywhere,
        scratch_shapes=[
            pltpu.VMEM((HEADS, MEMBERS, PIECE, QW), jnp.bfloat16),
            pltpu.VMEM((PLANES, HEADS, 2, MEMBERS, PIECE, HEAD), jnp.bfloat16),
            pltpu.VMEM((HEADS, MEMBERS, PIECE, QW), jnp.bfloat16),
            pltpu.VMEM((1, 2), jnp.int32),
            pltpu.VMEM((HEADS, RATIO, ROWS, HEAD), jnp.bfloat16),
            pltpu.VMEM((HEADS, RATIO, ROWS, HEAD), jnp.float32),
            pltpu.VMEM((HEADS, RATIO, ROWS, HEAD), jnp.float32),
            pltpu.VMEM((HEADS, RATIO, ROWS, HEAD), jnp.float32),
            dma,
            dma((HEADS,)),
            dma,
            dma((HEADS,)),
            dma((2, 4, HEADS)),
            dma((2, 4, HEADS)),
            dma,
            dma,
            dma,
            dma,
        ],
        compiler_params=pltpu.CompilerParams(
            collective_id=0, has_side_effects=True, vmem_limit_bytes=60 << 20
        ),
        cost_estimate=pl.CostEstimate(
            flops=pairs * HEADS * RATIO * HEAD * 4,
            bytes_accessed=16 << 20,
            transcendentals=pairs * HEADS * RATIO,
        ),
        name="attend_plane",
    )(query_rows, key_rows, value_row_array, lengths)


def solution(mesh):
    rows = P("grp", "sp", None, None, None)
    return jax.shard_map(
        on_device,
        mesh=mesh,
        in_specs=(rows, rows, rows, P("grp", None)),
        out_specs=rows,
        check_vma=False,
    )
```

```python
import functools

import jax
import jax.numpy as jnp
from jax import lax
from jax.experimental import pallas as pl
from jax.experimental.pallas import tpu as pltpu
from jax.sharding import PartitionSpec as P

MESH = pl.DeviceIdType.MESH
HEAD = 128
RATIO = 5
HEADS = 8
PLANES = 8
MEMBERS = 32
PIECE = 8
ROWS = MEMBERS * PIECE
STRIDE = 13
QW = RATIO * HEAD
HALF = 1024
FAR = 1e30
RATE = HEAD**-0.5 * 1.4426950408889634


def member(plane, j):
    return (plane * 4 + j // 8, j % 8)


def kernel(
    q_ref,
    k_ref,
    v_ref,
    len_ref,
    out_ref,
    qbuf,
    kv,
    obuf,
    ends,
    qh,
    top,
    total,
    acc,
    q_send,
    q_recv,
    kv_send,
    kv_recv,
    z_send,
    z_recv,
    o_send,
    o_recv,
    l_send,
    l_recv,
):
    g, s = lax.axis_index("grp"), lax.axis_index("sp")
    z, j = g // 4, (g % 4) * 8 + s
    up, down = member((z + 1) % 8, j), member((z + 7) % 8, j)

    barrier = pltpu.get_barrier_semaphore()

    def greet(i, _):
        pl.semaphore_signal(
            barrier, inc=1, device_id=member(z, (j + i) % MEMBERS), device_id_type=MESH
        )
        return 0

    lax.fori_loop(1, MEMBERS, greet, 0)
    pl.semaphore_signal(barrier, inc=1, device_id=up, device_id_type=MESH)
    pl.semaphore_signal(barrier, inc=1, device_id=down, device_id_type=MESH)
    to_plane, to_j = s, g
    alone = jnp.logical_and(to_plane == z, to_j == j)

    @pl.when(jnp.logical_not(alone))
    def _():
        pl.semaphore_signal(barrier, inc=1, device_id=(j, z), device_id_type=MESH)
        pl.semaphore_wait(barrier, MEMBERS + 2)

    @pl.when(alone)
    def _():
        pl.semaphore_wait(barrier, MEMBERS + 1)

    def send_kv(m):
        cols = pl.ds(pl.multiple_of(m * HEAD, HEAD), HEAD)

        def one(i, _):
            p = (j + i * STRIDE) % MEMBERS
            for n, ref in enumerate((k_ref, v_ref)):
                pltpu.make_async_remote_copy(
                    src_ref=ref.at[0, 0, p, :, cols],
                    dst_ref=kv.at[z, m, n, j],
                    send_sem=kv_send,
                    recv_sem=kv_recv.at[m],
                    device_id=member(z, p),
                    device_id_type=MESH,
                ).start()
            return 0

        lax.fori_loop(1, MEMBERS, one, 0)
        for n, ref in enumerate((k_ref, v_ref)):
            pltpu.make_async_copy(
                ref.at[0, 0, j, :, cols], kv.at[z, m, n, j], kv_recv.at[m]
            ).start()

    def send_q(m):
        cols = pl.ds(pl.multiple_of(m * QW, HEAD), QW)

        def one(i, _):
            p = (j + i * STRIDE) % MEMBERS
            pltpu.make_async_remote_copy(
                src_ref=q_ref.at[0, 0, p, :, cols],
                dst_ref=qbuf.at[m, j],
                send_sem=q_send,
                recv_sem=q_recv.at[m],
                device_id=member(z, p),
                device_id_type=MESH,
            ).start()
            return 0

        lax.fori_loop(1, MEMBERS, one, 0)
        pltpu.make_async_copy(
            q_ref.at[0, 0, j, :, cols], qbuf.at[m, j], q_recv.at[m]
        ).start()

    def send_out(m):
        cols = pl.ds(pl.multiple_of(m * QW, HEAD), QW)

        def one(i, _):
            p = (j + i * STRIDE) % MEMBERS
            pltpu.make_async_remote_copy(
                src_ref=obuf.at[m, p],
                dst_ref=out_ref.at[0, 0, j, :, cols],
                send_sem=o_send,
                recv_sem=o_recv,
                device_id=member(z, p),
                device_id_type=MESH,
            ).start()
            return 0

        lax.fori_loop(1, MEMBERS, one, 0)
        pltpu.make_async_copy(
            obuf.at[m, j], out_ref.at[0, 0, j, :, cols], o_recv
        ).start()

    def wait_bytes(ref, sem):
        pltpu.make_async_copy(ref, ref, sem).wait()

    def up_copy(b, m, hop):
        return pltpu.make_async_remote_copy(
            src_ref=kv.at[b, m],
            dst_ref=kv.at[b, m],
            send_sem=z_send.at[0, hop, m],
            recv_sem=z_recv.at[0, hop, m],
            device_id=up,
            device_id_type=MESH,
        )

    def down_copy(b, m, hop):
        return pltpu.make_async_remote_copy(
            src_ref=kv.at[b, m],
            dst_ref=kv.at[b, m],
            send_sem=z_send.at[1, hop, m],
            recv_sem=z_recv.at[1, hop, m],
            device_id=down,
            device_id_type=MESH,
        )

    def inside(m):
        return jnp.logical_and(m >= 0, m < HEADS)

    def all_of(*conditions):
        return functools.reduce(jnp.logical_and, conditions)

    def goes_up(b, m, hop):
        turn = all_of(hop == 3, b == 3, m % 2 == 0)
        return all_of(inside(m), b >= 0, b + hop < 7, jnp.logical_or(hop < 3, turn))

    def goes_down(b, m, hop):
        turn = jnp.logical_and(b == 3, m % 2 == 1)
        return all_of(inside(m), hop < 4, jnp.logical_or(b < 3, turn))

    def sends_up(m, hop):
        return goes_up(z - hop, m, hop)

    def sends_down(m, hop):
        return goes_down((z + hop) % 8, m, hop)

    def gets_up(m, hop):
        return goes_up(z - hop - 1, m, hop)

    def gets_down(m, hop):
        return goes_down((z + hop + 1) % 8, m, hop)

    def start_own(m):
        wait_bytes(kv.at[z, m], kv_recv.at[m])

        @pl.when(sends_up(m, 0))
        def _():
            up_copy(z, m, 0).start()

        @pl.when(sends_down(m, 0))
        def _():
            down_copy(z, m, 0).start()

    def flat(x):
        return x.astype(jnp.float32).reshape(ROWS, HEAD).astype(jnp.bfloat16)

    ones = jnp.ones((ROWS, HEAD), jnp.bfloat16)

    def scores_of(m, i, keys):
        return lax.dot_general(
            qh[m, i], keys, (((1,), (1,)), ((), ())), preferred_element_type=jnp.float32
        )

    def attend_own(m):
        keys = flat(kv[z, m, 0])
        values = jnp.concatenate([flat(kv[z, m, 1]), ones], axis=1)
        rows = lax.broadcasted_iota(jnp.int32, (ROWS, ROWS), 0)
        columns = lax.broadcasted_iota(jnp.int32, (ROWS, ROWS), 1)
        for i in range(RATIO):
            qh[m, i] = flat(qbuf[m, :, :, i * HEAD : (i + 1) * HEAD])
            scores = jnp.where(columns <= rows, scores_of(m, i, keys), -FAR)
            highest = jnp.max(scores, axis=1, keepdims=True)
            weights = jnp.exp2((scores - highest) * RATE).astype(jnp.bfloat16)
            both = jnp.dot(weights, values, preferred_element_type=jnp.float32)
            top[m, i] = jnp.broadcast_to(highest, (ROWS, HEAD))
            acc[m, i] = both[:, :HEAD]
            total[m, i] = both[:, HEAD:]

    def attend(m, b):
        keys = flat(kv[b, m, 0])
        values = jnp.concatenate([flat(kv[b, m, 1]), ones], axis=1)
        across = jnp.logical_and(z >= 4, b < 4).astype(jnp.int32)
        first = jnp.broadcast_to(ends[0:1, 0:1], (1, HEAD))
        hidden = jnp.where(first * across == HALF, -FAR, 0.0)
        for i in range(RATIO):
            scores = scores_of(m, i, keys)
            old = top[m, i]
            highest = jnp.max(scores, axis=1, keepdims=True) + hidden
            new = jnp.maximum(old, highest)
            shift = new - hidden
            weights = jnp.exp2(
                (scores - jnp.concatenate([shift, shift], axis=1)) * RATE
            ).astype(jnp.bfloat16)
            both = jnp.dot(weights, values, preferred_element_type=jnp.float32)
            shrink = jnp.exp2((old - new) * RATE)
            top[m, i] = new
            acc[m, i] = acc[m, i] * shrink + both[:, :HEAD]
            total[m, i] = total[m, i] * shrink + both[:, HEAD:]

    def finish(m):
        for i in range(RATIO):
            mixed = acc[m, i] / total[m, i]
            obuf[m, :, :, i * HEAD : (i + 1) * HEAD] = mixed.reshape(
                MEMBERS, PIECE, HEAD
            ).astype(jnp.bfloat16)

    len_copy = pltpu.make_async_remote_copy(
        src_ref=len_ref,
        dst_ref=ends,
        send_sem=l_send,
        recv_sem=l_recv,
        device_id=member(to_plane, to_j),
        device_id_type=MESH,
    )

    send_kv(0)

    @pl.when(jnp.logical_not(alone))
    def _():
        len_copy.start()

    @pl.when(alone)
    def _():
        pltpu.make_async_copy(len_ref, ends, l_recv).start()

    send_kv(1)
    send_kv(2)
    send_q(0)
    start_own(0)
    send_kv(3)
    send_q(1)

    def tick(t, _):
        @pl.when(t + 1 < HEADS)
        def _():
            start_own(t + 1)

        @pl.when(t == 0)
        def _():
            wait_bytes(ends, l_recv)

        def hop_step(hop, _):
            m = t - 1 - hop
            from_up = z - hop - 1
            from_down = (z + hop + 1) % 8

            @pl.when(gets_up(m, hop))
            def _():
                up_copy(from_up, m, hop).wait_recv()

                @pl.when(sends_up(m, hop + 1))
                def _():
                    up_copy(from_up, m, hop + 1).start()

            @pl.when(gets_down(m, hop))
            def _():
                down_copy(from_down, m, hop).wait_recv()

                @pl.when(sends_down(m, hop + 1))
                def _():
                    down_copy(from_down, m, hop + 1).start()

            @pl.when(jnp.logical_and(hop == 0, inside(t - 1)))
            def _():
                wait_bytes(qbuf.at[t - 1], q_recv.at[t - 1])
                attend_own(t - 1)

            @pl.when(gets_up(m, hop))
            def _():
                attend(m, from_up)

            @pl.when(jnp.logical_and(gets_down(m, hop), from_down < z))
            def _():
                attend(m, from_down)

            return 0

        lax.fori_loop(0, 4, hop_step, 0)

        @pl.when(t + 4 < HEADS)
        def _():
            send_kv(t + 4)

        @pl.when(t + 2 < HEADS)
        def _():
            send_q(t + 2)

        @pl.when(t >= 4)
        def _():
            finish(t - 4)
            send_out(t - 4)

        return 0

    lax.fori_loop(0, HEADS + 4, tick, 0)

    def drain(m, _):
        for hop in range(4):

            @pl.when(sends_up(m, hop))
            def _():
                up_copy(z, m, hop).wait_send()

            @pl.when(sends_down(m, hop))
            def _():
                down_copy(z, m, hop).wait_send()

        return 0

    lax.fori_loop(0, HEADS, drain, 0)

    @pl.when(jnp.logical_not(alone))
    def _():
        len_copy.wait_send()

    wait_bytes(kv.at[0, :, :, pl.ds(0, MEMBERS - 1)], kv_send)
    wait_bytes(qbuf.at[:, pl.ds(0, MEMBERS - 1)], q_send)
    wait_bytes(obuf.at[:, pl.ds(0, MEMBERS - 1)], o_send)
    wait_bytes(out_ref, o_recv)


def on_device(*arguments):
    query_rows = arguments[0]
    anywhere = pl.BlockSpec(memory_space=pl.ANY)
    there = pl.BlockSpec(memory_space=pltpu.HBM)
    dma = pltpu.SemaphoreType.DMA
    pairs = ROWS * ROWS * 8
    return pl.pallas_call(
        kernel,
        out_shape=jax.ShapeDtypeStruct(query_rows.shape, query_rows.dtype),
        in_specs=[there] * 4,
        out_specs=anywhere,
        scratch_shapes=[
            pltpu.VMEM((HEADS, MEMBERS, PIECE, QW), jnp.bfloat16),
            pltpu.VMEM((PLANES, HEADS, 2, MEMBERS, PIECE, HEAD), jnp.bfloat16),
            pltpu.VMEM((HEADS, MEMBERS, PIECE, QW), jnp.bfloat16),
            pltpu.VMEM((1, 2), jnp.int32),
            pltpu.VMEM((HEADS, RATIO, ROWS, HEAD), jnp.bfloat16),
            pltpu.VMEM((HEADS, RATIO, ROWS, HEAD), jnp.float32),
            pltpu.VMEM((HEADS, RATIO, ROWS, HEAD), jnp.float32),
            pltpu.VMEM((HEADS, RATIO, ROWS, HEAD), jnp.float32),
            dma,
            dma((HEADS,)),
            dma,
            dma((HEADS,)),
            dma((2, 4, HEADS)),
            dma((2, 4, HEADS)),
            dma,
            dma,
            dma,
            dma,
        ],
        compiler_params=pltpu.CompilerParams(
            collective_id=0, has_side_effects=True, vmem_limit_bytes=48 << 20
        ),
        cost_estimate=pl.CostEstimate(
            flops=pairs * HEADS * RATIO * HEAD * 4,
            bytes_accessed=16 << 20,
            transcendentals=pairs * HEADS * RATIO,
        ),
        name="attend_plane",
    )(*[pltpu.with_memory_space_constraint(x, pltpu.HBM) for x in arguments])


def solution(mesh):
    rows = P("grp", "sp", None, None, None)
    return jax.shard_map(
        on_device,
        mesh=mesh,
        in_specs=(rows, rows, rows, P("grp", None)),
        out_specs=rows,
        check_vma=False,
    )
```

```python
import functools

import jax
import jax.numpy as jnp
from jax import lax
from jax.experimental import pallas as pl
from jax.experimental.pallas import tpu as pltpu
from jax.sharding import PartitionSpec as P

MESH = pl.DeviceIdType.MESH
HEAD = 128
RATIO = 5
HEADS = 8
PLANES = 8
MEMBERS = 32
PIECE = 8
ROWS = MEMBERS * PIECE
STRIDE = 13
QW = RATIO * HEAD
HALF = 1024
FAR = 1e30
RATE = HEAD**-0.5 * 1.4426950408889634


def member(plane, j):
    return (plane * 4 + j // 8, j % 8)


def kernel(
    q_ref,
    k_ref,
    v_ref,
    len_ref,
    out_ref,
    qbuf,
    kv,
    obuf,
    ends,
    qh,
    top,
    total,
    acc,
    q_send,
    q_recv,
    kv_send,
    kv_recv,
    z_send,
    z_recv,
    o_send,
    o_recv,
    l_send,
    l_recv,
):
    g, s = lax.axis_index("grp"), lax.axis_index("sp")
    z, j = g // 4, (g % 4) * 8 + s
    up, down = member((z + 1) % 8, j), member((z + 7) % 8, j)

    barrier = pltpu.get_barrier_semaphore()

    def greet(i, _):
        pl.semaphore_signal(
            barrier, inc=1, device_id=member(z, (j + i) % MEMBERS), device_id_type=MESH
        )
        return 0

    lax.fori_loop(1, MEMBERS, greet, 0)
    pl.semaphore_signal(barrier, inc=1, device_id=up, device_id_type=MESH)
    pl.semaphore_signal(barrier, inc=1, device_id=down, device_id_type=MESH)
    to_plane, to_j = s, g
    alone = jnp.logical_and(to_plane == z, to_j == j)

    @pl.when(jnp.logical_not(alone))
    def _():
        pl.semaphore_signal(barrier, inc=1, device_id=(j, z), device_id_type=MESH)
        pl.semaphore_wait(barrier, MEMBERS + 2)

    @pl.when(alone)
    def _():
        pl.semaphore_wait(barrier, MEMBERS + 1)

    def send_kv(m):
        cols = pl.ds(pl.multiple_of(m * HEAD, HEAD), HEAD)

        def one(i, _):
            p = (j + i * STRIDE) % MEMBERS
            for n, ref in enumerate((k_ref, v_ref)):
                pltpu.make_async_remote_copy(
                    src_ref=ref.at[0, 0, p, :, cols],
                    dst_ref=kv.at[z, m, n, j],
                    send_sem=kv_send,
                    recv_sem=kv_recv.at[m],
                    device_id=member(z, p),
                    device_id_type=MESH,
                ).start()
            return 0

        lax.fori_loop(1, MEMBERS, one, 0)
        for n, ref in enumerate((k_ref, v_ref)):
            pltpu.make_async_copy(
                ref.at[0, 0, j, :, cols], kv.at[z, m, n, j], kv_recv.at[m]
            ).start()

    def send_q(m):
        cols = pl.ds(pl.multiple_of(m * QW, HEAD), QW)

        def one(i, _):
            p = (j + i * STRIDE) % MEMBERS
            pltpu.make_async_remote_copy(
                src_ref=q_ref.at[0, 0, p, :, cols],
                dst_ref=qbuf.at[m, j],
                send_sem=q_send,
                recv_sem=q_recv.at[m],
                device_id=member(z, p),
                device_id_type=MESH,
            ).start()
            return 0

        lax.fori_loop(1, MEMBERS, one, 0)
        pltpu.make_async_copy(
            q_ref.at[0, 0, j, :, cols], qbuf.at[m, j], q_recv.at[m]
        ).start()

    def send_out(m):
        cols = pl.ds(pl.multiple_of(m * QW, HEAD), QW)

        def one(i, _):
            p = (j + i * STRIDE) % MEMBERS
            pltpu.make_async_remote_copy(
                src_ref=obuf.at[m, p],
                dst_ref=out_ref.at[0, 0, j, :, cols],
                send_sem=o_send,
                recv_sem=o_recv,
                device_id=member(z, p),
                device_id_type=MESH,
            ).start()
            return 0

        lax.fori_loop(1, MEMBERS, one, 0)
        pltpu.make_async_copy(
            obuf.at[m, j], out_ref.at[0, 0, j, :, cols], o_recv
        ).start()

    def wait_bytes(ref, sem):
        pltpu.make_async_copy(ref, ref, sem).wait()

    def up_copy(b, m, hop):
        return pltpu.make_async_remote_copy(
            src_ref=kv.at[b, m],
            dst_ref=kv.at[b, m],
            send_sem=z_send.at[0, hop, m],
            recv_sem=z_recv.at[0, hop, m],
            device_id=up,
            device_id_type=MESH,
        )

    def down_copy(b, m, hop):
        return pltpu.make_async_remote_copy(
            src_ref=kv.at[b, m],
            dst_ref=kv.at[b, m],
            send_sem=z_send.at[1, hop, m],
            recv_sem=z_recv.at[1, hop, m],
            device_id=down,
            device_id_type=MESH,
        )

    def inside(m):
        return jnp.logical_and(m >= 0, m < HEADS)

    def all_of(*conditions):
        return functools.reduce(jnp.logical_and, conditions)

    def goes_up(b, m, hop):
        turn = all_of(hop == 3, b == 3, m % 2 == 0)
        return all_of(inside(m), b >= 0, b + hop < 7, jnp.logical_or(hop < 3, turn))

    def goes_down(b, m, hop):
        turn = jnp.logical_and(b == 3, m % 2 == 1)
        return all_of(inside(m), hop < 4, jnp.logical_or(b < 3, turn))

    def sends_up(m, hop):
        return goes_up(z - hop, m, hop)

    def sends_down(m, hop):
        return goes_down((z + hop) % 8, m, hop)

    def gets_up(m, hop):
        return goes_up(z - hop - 1, m, hop)

    def gets_down(m, hop):
        return goes_down((z + hop + 1) % 8, m, hop)

    def start_own(m):
        wait_bytes(kv.at[z, m], kv_recv.at[m])

        @pl.when(sends_up(m, 0))
        def _():
            up_copy(z, m, 0).start()

        @pl.when(sends_down(m, 0))
        def _():
            down_copy(z, m, 0).start()

    def flat(x):
        return x.astype(jnp.float32).reshape(ROWS, HEAD).astype(jnp.bfloat16)

    ones = jnp.ones((ROWS, HEAD), jnp.bfloat16)

    def scores_of(m, i, keys):
        return lax.dot_general(
            qh[m, i], keys, (((1,), (1,)), ((), ())), preferred_element_type=jnp.float32
        )

    def attend_own(m):
        keys = flat(kv[z, m, 0])
        values = jnp.concatenate([flat(kv[z, m, 1]), ones], axis=1)
        rows = lax.broadcasted_iota(jnp.int32, (ROWS, ROWS), 0)
        columns = lax.broadcasted_iota(jnp.int32, (ROWS, ROWS), 1)
        for i in range(RATIO):
            qh[m, i] = flat(qbuf[m, :, :, i * HEAD : (i + 1) * HEAD])
            scores = jnp.where(columns <= rows, scores_of(m, i, keys), -FAR)
            highest = jnp.max(scores, axis=1, keepdims=True)
            weights = jnp.exp2((scores - highest) * RATE).astype(jnp.bfloat16)
            both = jnp.dot(weights, values, preferred_element_type=jnp.float32)
            top[m, i] = jnp.broadcast_to(highest, (ROWS, HEAD))
            acc[m, i] = both[:, :HEAD]
            total[m, i] = both[:, HEAD:]

    def attend(m, b):
        keys = flat(kv[b, m, 0])
        values = jnp.concatenate([flat(kv[b, m, 1]), ones], axis=1)
        across = jnp.logical_and(z >= 4, b < 4).astype(jnp.int32)
        first = jnp.broadcast_to(ends[0:1, 0:1], (1, HEAD))
        hidden = jnp.where(first * across == HALF, -FAR, 0.0)
        for i in range(RATIO):
            scores = scores_of(m, i, keys)
            old = top[m, i]
            highest = jnp.max(scores, axis=1, keepdims=True) + hidden
            new = jnp.maximum(old, highest)
            shift = new - hidden
            weights = jnp.exp2(
                (scores - jnp.concatenate([shift, shift], axis=1)) * RATE
            ).astype(jnp.bfloat16)
            both = jnp.dot(weights, values, preferred_element_type=jnp.float32)
            shrink = jnp.exp2((old - new) * RATE)
            top[m, i] = new
            acc[m, i] = acc[m, i] * shrink + both[:, :HEAD]
            total[m, i] = total[m, i] * shrink + both[:, HEAD:]

    def finish(m):
        for i in range(RATIO):
            mixed = acc[m, i] / total[m, i]
            obuf[m, :, :, i * HEAD : (i + 1) * HEAD] = mixed.reshape(
                MEMBERS, PIECE, HEAD
            ).astype(jnp.bfloat16)

    len_copy = pltpu.make_async_remote_copy(
        src_ref=len_ref,
        dst_ref=ends,
        send_sem=l_send,
        recv_sem=l_recv,
        device_id=member(to_plane, to_j),
        device_id_type=MESH,
    )

    send_kv(0)

    @pl.when(jnp.logical_not(alone))
    def _():
        len_copy.start()

    @pl.when(alone)
    def _():
        pltpu.make_async_copy(len_ref, ends, l_recv).start()

    send_kv(1)
    send_kv(2)
    send_q(0)
    start_own(0)
    send_kv(3)
    send_q(1)

    def tick(t, _):
        @pl.when(t + 1 < HEADS)
        def _():
            start_own(t + 1)

        @pl.when(t == 0)
        def _():
            wait_bytes(ends, l_recv)

        def hop_step(hop, _):
            m = t - 1 - hop
            from_up = z - hop - 1
            from_down = (z + hop + 1) % 8

            @pl.when(gets_down(m, hop))
            def _():
                down_copy(from_down, m, hop).wait_recv()

                @pl.when(sends_down(m, hop + 1))
                def _():
                    down_copy(from_down, m, hop + 1).start()

            @pl.when(gets_up(m, hop))
            def _():
                up_copy(from_up, m, hop).wait_recv()

                @pl.when(sends_up(m, hop + 1))
                def _():
                    up_copy(from_up, m, hop + 1).start()

            @pl.when(jnp.logical_and(hop == 0, inside(t - 1)))
            def _():
                wait_bytes(qbuf.at[t - 1], q_recv.at[t - 1])
                attend_own(t - 1)

            @pl.when(gets_up(m, hop))
            def _():
                attend(m, from_up)

            @pl.when(jnp.logical_and(gets_down(m, hop), from_down < z))
            def _():
                attend(m, from_down)

            return 0

        lax.fori_loop(0, 4, hop_step, 0)

        @pl.when(t + 4 < HEADS)
        def _():
            send_kv(t + 4)

        @pl.when(t + 2 < HEADS)
        def _():
            send_q(t + 2)

        @pl.when(t >= 4)
        def _():
            finish(t - 4)
            send_out(t - 4)

        return 0

    lax.fori_loop(0, HEADS + 4, tick, 0)

    def drain(m, _):
        for hop in range(4):

            @pl.when(sends_up(m, hop))
            def _():
                up_copy(z, m, hop).wait_send()

            @pl.when(sends_down(m, hop))
            def _():
                down_copy(z, m, hop).wait_send()

        return 0

    lax.fori_loop(0, HEADS, drain, 0)

    @pl.when(jnp.logical_not(alone))
    def _():
        len_copy.wait_send()

    wait_bytes(kv.at[0, :, :, pl.ds(0, MEMBERS - 1)], kv_send)
    wait_bytes(qbuf.at[:, pl.ds(0, MEMBERS - 1)], q_send)
    wait_bytes(obuf.at[:, pl.ds(0, MEMBERS - 1)], o_send)
    wait_bytes(out_ref, o_recv)


def on_device(*arguments):
    query_rows = arguments[0]
    anywhere = pl.BlockSpec(memory_space=pl.ANY)
    there = pl.BlockSpec(memory_space=pltpu.HBM)
    dma = pltpu.SemaphoreType.DMA
    pairs = ROWS * ROWS * 8
    return pl.pallas_call(
        kernel,
        out_shape=jax.ShapeDtypeStruct(query_rows.shape, query_rows.dtype),
        in_specs=[there] * 4,
        out_specs=anywhere,
        scratch_shapes=[
            pltpu.VMEM((HEADS, MEMBERS, PIECE, QW), jnp.bfloat16),
            pltpu.VMEM((PLANES, HEADS, 2, MEMBERS, PIECE, HEAD), jnp.bfloat16),
            pltpu.VMEM((HEADS, MEMBERS, PIECE, QW), jnp.bfloat16),
            pltpu.VMEM((1, 2), jnp.int32),
            pltpu.VMEM((HEADS, RATIO, ROWS, HEAD), jnp.bfloat16),
            pltpu.VMEM((HEADS, RATIO, ROWS, HEAD), jnp.float32),
            pltpu.VMEM((HEADS, RATIO, ROWS, HEAD), jnp.float32),
            pltpu.VMEM((HEADS, RATIO, ROWS, HEAD), jnp.float32),
            dma,
            dma((HEADS,)),
            dma,
            dma((HEADS,)),
            dma((2, 4, HEADS)),
            dma((2, 4, HEADS)),
            dma,
            dma,
            dma,
            dma,
        ],
        compiler_params=pltpu.CompilerParams(
            collective_id=0, has_side_effects=True, vmem_limit_bytes=48 << 20
        ),
        cost_estimate=pl.CostEstimate(
            flops=pairs * HEADS * RATIO * HEAD * 4,
            bytes_accessed=16 << 20,
            transcendentals=pairs * HEADS * RATIO,
        ),
        name="attend_plane",
    )(*[pltpu.with_memory_space_constraint(x, pltpu.HBM) for x in arguments])


def solution(mesh):
    rows = P("grp", "sp", None, None, None)
    return jax.shard_map(
        on_device,
        mesh=mesh,
        in_specs=(rows, rows, rows, P("grp", None)),
        out_specs=rows,
        check_vma=False,
    )
```
